256 devices in a mesh: tm: 256 (over x, y, z, core).
Axes of the slice: x: 4, y: 4, z: 8, core: 2. Of those that a mesh axis runs over, the one named last changes fastest.
Arguments:
- samples: float32 [256, 2, 256, 256], P('tm'), may hold values from -0.5 to 0.5
Outputs:
- propagators: float32 [256, 2, 256, 256], P('tm')
The draws below stay inside these ranges and needn't reach their ends.
All inputs are finite; a program needn't handle non-finite values.
Results may differ from the reference program's by a relative error of at most 0.0003.
Values sent between devices are 32-bit elements; how exact they have to be, the bound alone decides.
A program may use at most 64 MiB of HBM per device.

```python
import jax
import jax.numpy as jnp
from jax import lax

D = 256
SLICES = 256


def steps_of(key, extent, shards, low, largest):
    def one(position, shards_of):
        heights = jax.random.uniform(jax.random.fold_in(jax.random.fold_in(key, 6), position), (shards_of,), jnp.float32, low / len(shards), largest / len(shards))
        return jnp.repeat(jnp.exp(heights), extent[position] // shards_of).reshape((-1,) + (1,) * (len(extent) - position - 1))

    loudness = one(*shards[0])
    for cut in shards[1:]:
        loudness = loudness * one(*cut)
    return loudness


def centred(rng, shape, width, most, cuts=(), kind=jnp.bfloat16):
    array = width * jax.random.normal(rng, shape, jnp.float32)
    if cuts:
        array = array * steps_of(rng, shape, cuts, -0.22, 0.18)
    return jnp.clip(array, -most, most).astype(kind)


def setup_inputs(seed: int = 0) -> dict:
    seeds = jax.random.split(jax.random.key(seed), 2)
    samples = centred(seeds[0], (SLICES, 2, D, D), (4 * D // 9) ** -0.5, 0.5, ((0, 256),), jnp.float32)
    return {"samples": samples}


time_step = 0.25


def complex_product(left, right):
    size = left.shape[-1]
    joined = jnp.concatenate([right[0], right[1]], axis=1)
    real_rows = jnp.dot(left[0], joined, preferred_element_type=jnp.float32, precision=lax.Precision.HIGHEST)
    imag_rows = jnp.dot(left[1], joined, preferred_element_type=jnp.float32, precision=lax.Precision.HIGHEST)
    real_part = real_rows[:, :size] - imag_rows[:, size:]
    imag_part = real_rows[:, size:] + imag_rows[:, :size]
    return jnp.stack([real_part, imag_part])


def hermitian(drawn):
    return jnp.stack([(drawn[0] + drawn[0].T) * 0.5, (drawn[1] - drawn[1].T) * 0.5])


def unit_matrix(size):
    return jnp.stack([jnp.eye(size, dtype=jnp.float32), jnp.zeros((size, size), jnp.float32)])


def magnus_factor(first, second):
    size = first.shape[-1]
    summed = first + second
    product = complex_product(second, first)
    comm_real = product[0] - product[0].T
    comm_imag = product[1] + product[1].T
    shrink = time_step * time_step / 12.0
    omega = jnp.stack([0.5 * time_step * summed[1] - shrink * comm_real,
                       -0.5 * time_step * summed[0] - shrink * comm_imag])
    identity = unit_matrix(size)
    nested = identity + omega / 4.0
    nested = identity + complex_product(omega, nested) / 3.0
    nested = identity + complex_product(omega, nested) / 2.0
    return identity + complex_product(omega, nested)


def reference(samples):
    current = jax.vmap(hermitian)(samples)
    following = jnp.roll(current, -1, axis=0)
    factors = lax.map(lambda pair: magnus_factor(pair[0], pair[1]), (current, following))

    def advance(carry, factor):
        fresh = complex_product(factor, carry)
        return fresh, fresh

    start = unit_matrix(samples.shape[-1])
    _, cumulative = lax.scan(advance, start, factors)
    return cumulative
```

```python
import functools

import jax
import jax.numpy as jnp
from jax import lax
from jax.experimental import pallas as pl
from jax.experimental.pallas import tpu as pltpu
from jax.sharding import PartitionSpec as P

MESH = pl.DeviceIdType.MESH
time_step = 0.25
SLABS = 4


def halves(x):
    high = x.astype(jnp.bfloat16)
    return high, (x - high.astype(jnp.float32)).astype(jnp.bfloat16)


def dot(a, b):
    return jnp.dot(a, b, preferred_element_type=jnp.float32)


def product(x, high, low):
    m = x.shape[0]
    xh, xl = halves(x)
    both = jnp.concatenate([xh, xl], axis=0)
    by_real = dot(both, high[0])
    by_imag = dot(both, high[1])
    by_real = by_real[:m] + by_real[m:] + dot(xh, low[0])
    by_imag = by_imag[:m] + by_imag[m:] + dot(xh, low[1])
    n = m // 2
    return by_real[:n] - by_imag[n:], by_imag[:n] + by_real[n:]


def each_slab(body):
    lax.fori_loop(0, SLABS, body, 0)


def kernel(
    devices, x_ref, o_ref,
    packed, packed_in, value, unit, keep, got, swap, last, high, low,
    h_send, h_recv, u_send, u_recv, g_send, g_recv, s_send, s_recv, f_send, f_recv,
):
    size = x_ref.shape[-1]
    width = size // (2 * SLABS)
    chips = devices // 2
    me = lax.axis_index("tm")
    core = lax.rem(me, 2)
    chip = me // 2
    other = me + 1 - 2 * core
    before = lax.rem(me + devices - 1, devices)
    after = lax.rem(me + 1, devices)

    stages = []
    shift = 1
    while shift < chips:
        stages.append((shift, chip >= shift, chip + shift < chips))
        shift *= 2
    n_stages = len(stages)

    barrier = pltpu.get_barrier_semaphore()

    def greet(device):
        pl.semaphore_signal(barrier, inc=1, device_id=(device,), device_id_type=MESH)

    greet(other)
    greet(before)
    greet(after)
    expected = 3
    for shift, takes, gives in stages:
        pl.when(takes)(functools.partial(greet, me - 2 * shift))
        pl.when(gives)(functools.partial(greet, me + 2 * shift))
        expected = expected + takes.astype(jnp.int32) + gives.astype(jnp.int32)

    def remote(src, dst, send, recv, device):
        return pltpu.make_async_remote_copy(
            src_ref=src, dst_ref=dst, send_sem=send, recv_sem=recv,
            device_id=(device,), device_id_type=MESH,
        )

    row = lax.broadcasted_iota(jnp.int32, (size, size), 0)
    col = lax.broadcasted_iota(jnp.int32, (size, size), 1)
    h_real = (x_ref[0] + x_ref[0].T) * 0.5
    h_imag = (x_ref[1] - x_ref[1].T) * 0.5
    packed[...] = jnp.where(col >= row, h_real, h_imag)
    pl.semaphore_wait(barrier, expected)
    h_copy = remote(packed, packed_in, h_send, h_recv, before)
    h_copy.start()
    value[0] = h_real
    value[1] = h_imag
    for part, h in enumerate((h_real, h_imag)):
        high[0, 0, part], low[0, 0, part] = halves(h)
    h_copy.wait_recv()
    flat = packed_in[...]
    turned = flat.T
    n_real = jnp.where(col >= row, flat, turned)
    n_imag = jnp.where(row > col, flat, jnp.where(row < col, -turned, 0.0))
    x_real, x_imag = product(jnp.concatenate([n_real, n_imag], axis=0), high[0, 0], low[0, 0])
    shrink = time_step * time_step / 12.0
    m_real = shrink * (x_real - x_real.T) - 0.5 * time_step * (value[1] + n_imag)
    m_imag = -0.5 * time_step * (value[0] + n_real) - shrink * (x_imag + x_imag.T)
    for part, h in enumerate((m_real, m_imag)):
        high[0, 1, part], low[0, 1, part] = halves(h)
    eye = jnp.where(row == col, 1.0, 0.0)
    value[0] = eye + m_real * 0.25
    value[1] = m_imag * 0.25
    for divisor in (3.0, 2.0, 1.0):
        v_real, v_imag = product(
            jnp.concatenate([value[0], value[1]], axis=0), high[0, 1], low[0, 1]
        )
        if divisor == 1.0:
            value[0] = eye + v_real
            value[1] = v_imag
        else:
            value[0] = eye + v_real * (1.0 / divisor)
            value[1] = v_imag * (1.0 / divisor)
    for j in range(2 * SLABS):
        for part in range(2):
            unit[core, j, part] = value[part, j * width:(j + 1) * width]
    u_copy = remote(unit.at[core], unit.at[core], u_send, u_recv.at[core], other)
    u_copy.start()
    remote(unit.at[1 - core], unit.at[1 - core], u_send, u_recv.at[1 - core], other).wait_recv()

    for j in range(2 * SLABS):
        for part in range(2):
            rows = slice(j * width, (j + 1) * width)
            high[0, 0, part, rows], low[0, 0, part, rows] = halves(unit[1, j, part])
            high[1, 1, part, rows], low[1, 1, part, rows] = halves(unit[0, j, part])

    def give(s, j):
        shift = stages[s][0]
        return remote(keep.at[s, j, 0], got.at[s, j], g_send.at[s, j], g_recv.at[s, j], me + 2 * shift)

    def share(s, j, which):
        return remote(
            keep.at[s, j, which], swap.at[s, j, which],
            s_send.at[s, j, which], s_recv.at[s, j, which], other,
        )

    def finish(j):
        return remote(keep.at[n_stages, j, core], last.at[j], f_send.at[j], f_recv.at[j], other)

    def put(slot, which, first, part, value):
        rows = pl.ds(pl.multiple_of(first, width), width)
        high[slot, which, part, rows], low[slot, which, part, rows] = halves(value)

    def spread(s, j, which, real, imag):
        keep[s, j, which, 0] = real
        keep[s, j, which, 1] = imag
        if s < n_stages:
            first = core * (SLABS * width) + j * width
            put((s + 1) % 2, which, first, 0, real)
            put((s + 1) % 2, which, first, 1, imag)

    def chip_product(j, _):
        mine = core * SLABS + j
        x = unit[0, mine].reshape(2 * width, size)
        real, imag = product(x, high[0, 0], low[0, 0])
        spread(0, j, 0, real, imag)
        pl.when(stages[0][2])(lambda: give(0, j).start())
        share(0, j, 0).start()
        keep[0, j, 1] = unit[0, mine]
        return 0

    each_slab(chip_product)

    for s, (shift, takes, gives) in enumerate(stages):
        slot = (s + 1) % 2
        final = s + 1 == n_stages
        whichs = (0,) if s == 0 else (0, 1)

        def collect(j, _, s=s, slot=slot, whichs=whichs):
            for which in whichs:
                share(s, j, which).wait_recv()
                first = (1 - core) * (SLABS * width) + j * width
                put(slot, which, first, 0, swap[s, j, which, 0])
                put(slot, which, first, 1, swap[s, j, which, 1])
            return 0

        def take(j, _, s=s, slot=slot, final=final):
            give(s, j).wait_recv()
            x = got[s, j].reshape(2 * width, size)
            for which in (0, 1):
                real, imag = product(x, high[slot, which], low[slot, which])
                spread(s + 1, j, which, real, imag)
                if not final:
                    if which == 0:
                        pl.when(stages[s + 1][2])(lambda: give(s + 1, j).start())
                    share(s + 1, j, which).start()
            if final:
                finish(j).start()
            return 0

        def idle(j, _, s=s, final=final):
            keep[s + 1, j] = keep[s, j]
            if final:
                finish(j).start()
            else:
                pl.when(stages[s + 1][2])(lambda: give(s + 1, j).start())
            return 0

        if s == 0:
            each_slab(collect)
        else:
            pl.when(stages[s - 1][1])(functools.partial(each_slab, collect))
        pl.when(takes)(functools.partial(each_slab, take))
        pl.when(jnp.logical_not(takes))(functools.partial(each_slab, idle))

    def arrive(j, _):
        finish(j).wait_recv()
        for part in range(2):
            first = core * (SLABS * width) + j * width
            value[part, pl.ds(pl.multiple_of(first, width), width)] = keep[n_stages, j, 1 - core, part]
            first = (1 - core) * (SLABS * width) + j * width
            value[part, pl.ds(pl.multiple_of(first, width), width)] = last[j, part]
        return 0

    each_slab(arrive)
    o_ref[0] = value[0].T
    o_ref[1] = value[1].T

    h_copy.wait_send()
    u_copy.wait_send()

    def drain(j, _):
        for s, (shift, takes, gives) in enumerate(stages):
            pl.when(gives)(lambda s=s: give(s, j).wait_send())
            if s == 0:
                share(s, j, 0).wait_send()
            else:
                def both(s=s):
                    share(s, j, 0).wait_send()
                    share(s, j, 1).wait_send()
                pl.when(stages[s - 1][1])(both)
        finish(j).wait_send()
        return 0

    each_slab(drain)


def on_device(samples):
    x = samples[0]
    size = x.shape[-1]
    devices = lax.axis_size("tm")
    n_stages = (devices // 2).bit_length() - 1
    width = size // (2 * SLABS)
    f32, bf16 = jnp.float32, jnp.bfloat16
    slab = (2, width, size)
    dma = pltpu.SemaphoreType.DMA
    out = pl.pallas_call(
        functools.partial(kernel, devices),
        out_shape=jax.ShapeDtypeStruct(x.shape, f32),
        in_specs=[pl.BlockSpec(memory_space=pltpu.VMEM)],
        out_specs=pl.BlockSpec(memory_space=pltpu.VMEM),
        scratch_shapes=[
            pltpu.VMEM((size, size), f32),
            pltpu.VMEM((size, size), f32),
            pltpu.VMEM((2, size, size), f32),
            pltpu.VMEM((2, 2 * SLABS, *slab), f32),
            pltpu.VMEM((n_stages + 1, SLABS, 2, *slab), f32),
            pltpu.VMEM((n_stages, SLABS, *slab), f32),
            pltpu.VMEM((n_stages, SLABS, 2, *slab), f32),
            pltpu.VMEM((SLABS, *slab), f32),
            pltpu.VMEM((2, 2, 2, size, size), bf16),
            pltpu.VMEM((2, 2, 2, size, size), bf16),
            dma, dma, dma, dma((2,)),
            dma((n_stages, SLABS)), dma((n_stages, SLABS)),
            dma((n_stages, SLABS, 2)), dma((n_stages, SLABS, 2)),
            dma((SLABS,)), dma((SLABS,)),
        ],
        compiler_params=pltpu.CompilerParams(
            collective_id=0, has_side_effects=True, vmem_limit_bytes=48 << 20
        ),
        name="propagators",
    )(x)
    return out[None]


def solution(mesh):
    spec = P("tm", None, None, None)
    return jax.shard_map(on_device, mesh=mesh, in_specs=(spec,), out_specs=spec, check_vma=False)
```

```python
import functools

import jax
import jax.numpy as jnp
from jax import lax
from jax.experimental import pallas as pl
from jax.experimental.pallas import tpu as pltpu
from jax.sharding import PartitionSpec as P

MESH = pl.DeviceIdType.MESH
time_step = 0.25
WIDTH = 32
PARTS = 4


def halves(x):
    high = x.astype(jnp.bfloat16)
    return high, (x - high.astype(jnp.float32)).astype(jnp.bfloat16)


def dot(a, b):
    return jnp.dot(a, b, preferred_element_type=jnp.float32)


def product(x, high, low):
    m = x.shape[0]
    xh, xl = halves(x)
    both = jnp.concatenate([xh, xl], axis=0)
    by_real = dot(both, high[0])
    by_imag = dot(both, high[1])
    by_real = by_real[:m] + by_real[m:] + dot(xh, low[0])
    by_imag = by_imag[:m] + by_imag[m:] + dot(xh, low[1])
    n = m // 2
    return by_real[:n] - by_imag[n:], by_imag[:n] + by_real[n:]


def stacked(x):
    size = x.shape[-1]
    return jnp.concatenate([x[:, 0].reshape(-1, size), x[:, 1].reshape(-1, size)], axis=0)


def kernel(
    devices, x_ref, o_ref,
    drawn, packed, packed_in, value, unit, total, keep, got, swap, swap_second, last, crossed, high, low,
    x_sem, h_send, h_recv, u_send, u_recv, t_send, t_recv, p_send, p_recv, g_send, g_recv,
    s_send, s_recv, w_send, w_recv, f_send, f_recv, c_send, c_recv,
):
    size = x_ref.shape[-1]
    half = size // 2
    slabs = half // WIDTH
    per_part = slabs // PARTS
    chips = devices // 2
    me = lax.axis_index("tm")
    core = lax.rem(me, 2)
    chip = me // 2
    odd = lax.rem(chip, 2) == 1
    even = jnp.logical_not(odd)
    first_core = core == 0
    second_core = core == 1
    other = me + 1 - 2 * core
    before = lax.rem(me + devices - 1, devices)
    after = lax.rem(me + 1, devices)

    def device(chip, core):
        return chip * 2 + core

    shifts = []
    shift = 2
    while shift < chips:
        shifts.append(shift)
        shift *= 2
    n_shifts = len(shifts)
    takes = [odd] + [jnp.logical_and(odd, chip > by) for by in shifts]
    gives = [jnp.logical_and(odd, chip + by < chips) for by in shifts]
    gives_last = jnp.logical_and(odd, chip + 1 < chips)
    takes_last = jnp.logical_and(even, chip > 0)
    taken = sum(t.astype(jnp.int32) for t in takes)

    barrier = pltpu.get_barrier_semaphore()
    expected = 0

    def greet(when, device):
        @pl.when(when)
        def _():
            pl.semaphore_signal(barrier, inc=1, device_id=(device,), device_id_type=MESH)

        return when.astype(jnp.int32)

    always = chip >= 0
    pairs = [(always, other), (always, before), (always, after)]
    pairs += [(jnp.logical_and(even, second_core), device(chip + 1, c)) for c in range(2)]
    pairs += [(odd, device(chip - 1, 1))]
    for by, t, g in zip(shifts, takes[1:], gives):
        pairs += [(t, me - 2 * by), (g, me + 2 * by)]
    pairs += [(gives_last, me + 2), (takes_last, me - 2)]
    for when, where in pairs:
        expected = expected + greet(when, where)

    x_copy = pltpu.make_async_copy(x_ref, drawn, x_sem)
    x_copy.start()

    def remote(src, dst, send, recv, device):
        return pltpu.make_async_remote_copy(
            src_ref=src, dst_ref=dst, send_sem=send, recv_sem=recv,
            device_id=(device,), device_id_type=MESH,
        )

    row = lax.broadcasted_iota(jnp.int32, (size, size), 0)
    col = lax.broadcasted_iota(jnp.int32, (size, size), 1)
    x_copy.wait()
    h_real = (drawn[0] + drawn[0].T) * 0.5
    h_imag = (drawn[1] - drawn[1].T) * 0.5
    packed[...] = jnp.where(col >= row, h_real, h_imag)
    pl.semaphore_wait(barrier, expected)
    h_copy = remote(packed, packed_in, h_send, h_recv, before)
    h_copy.start()
    value[0] = h_real
    value[1] = h_imag
    for part, h in enumerate((h_real, h_imag)):
        high[0, 0, part], low[0, 0, part] = halves(h)
    h_copy.wait_recv()
    flat = packed_in[...]
    turned = flat.T
    n_real = jnp.where(col >= row, flat, turned)
    n_imag = jnp.where(row > col, flat, jnp.where(row < col, -turned, 0.0))
    x_real, x_imag = product(jnp.concatenate([n_real, n_imag], axis=0), high[0, 0], low[0, 0])
    shrink = time_step * time_step / 12.0
    m_real = shrink * (x_real - x_real.T) - 0.5 * time_step * (value[1] + n_imag)
    m_imag = -0.5 * time_step * (value[0] + n_real) - shrink * (x_imag + x_imag.T)
    for part, h in enumerate((m_real, m_imag)):
        high[0, 1, part], low[0, 1, part] = halves(h)

    def put(slot, which, first, part, value):
        rows = pl.ds(first, value.shape[0])
        high[slot, which, part, rows], low[slot, which, part, rows] = halves(value)

    u_copy = remote(unit, unit, u_send, u_recv, other)

    @pl.when(first_core)
    def _():
        eye = jnp.where(row == col, 1.0, 0.0)
        v_real = eye + m_real * 0.25
        v_imag = m_imag * 0.25
        for divisor in (3.0, 2.0, 1.0):
            v_real, v_imag = product(
                jnp.concatenate([v_real, v_imag], axis=0), high[0, 1], low[0, 1]
            )
            if divisor != 1.0:
                v_real = v_real * (1.0 / divisor)
                v_imag = v_imag * (1.0 / divisor)
            v_real = eye + v_real
        unit[:, 0] = v_real.reshape(2 * slabs, WIDTH, size)
        unit[:, 1] = v_imag.reshape(2 * slabs, WIDTH, size)
        u_copy.start()
        put(1, 1, 0, 0, v_real)
        put(1, 1, 0, 1, v_imag)

    def pair_give(part, side, j):
        slab = part * per_part + j
        return remote(
            total.at[part, side, j], got.at[0, slab], p_send.at[side, slab], p_recv.at[slab],
            device(chip + 1, side),
        )

    def total_copy(part):
        return remote(total.at[part], total.at[part], t_send.at[part], t_recv.at[part], other)

    @pl.when(second_core)
    def _():
        u_copy.wait_recv()
        for part in range(PARTS):
            span = slice(part * per_part, (part + 1) * per_part)
            sides = [unit[side * slabs + part * per_part:side * slabs + (part + 1) * per_part] for side in range(2)]
            y = stacked(jnp.concatenate(sides, axis=0))
            rows = y.shape[0] // 2
            z = y
            for divisor in (4.0, 3.0, 2.0, 1.0):
                z_real, z_imag = product(z, high[0, 1], low[0, 1])
                z = jnp.concatenate([z_real, z_imag], axis=0)
                if divisor != 1.0:
                    z = z * (1.0 / divisor)
                z = y + z
            for k in range(2):
                block = z[k * rows:(k + 1) * rows]
                total[part, :, :, k] = block.reshape(2, per_part, WIDTH, size)

            @pl.when(even)
            def _():
                for j in range(per_part):
                    for side in range(2):
                        pair_give(part, side, j).start()

            @pl.when(odd)
            def _():
                total_copy(part).start()

            for k in range(2):
                for side in range(2):
                    first = k * rows + side * (rows // 2)
                    put(1, 0, side * half + part * (rows // 2), k, z[first:first + rows // 2])

        @pl.when(odd)
        def _():
            for k in range(2):
                put(1, 1, 0, k, unit[:, k].reshape(size, size))

    @pl.when(jnp.logical_and(odd, first_core))
    def _():
        for part in range(PARTS):
            total_copy(part).wait_recv()
            for side in range(2):
                for k in range(2):
                    block = total[part, side, :, k].reshape(half // PARTS, size)
                    put(1, 0, side * half + part * (half // PARTS), k, block)

    mine = pl.multiple_of(core * half, half)
    theirs = pl.multiple_of((1 - core) * half, half)

    def give(s, j, by):
        return remote(
            keep.at[jnp.minimum(s, taken) - 1, 0, j], got.at[s, j], g_send.at[s, j], g_recv.at[s, j],
            me + 2 * by,
        )

    def share(s, j):
        return remote(keep.at[s, 0, j], swap.at[s, j], s_send.at[s, j], s_recv.at[s, j], other)

    def share_second(s):
        return remote(keep.at[s, 1], swap_second.at[s], w_send.at[s], w_recv.at[s], other)

    def finish():
        return remote(keep.at[taken - 1, core], last, f_send, f_recv, other)

    def cross(j):
        return remote(got.at[n_shifts + 1, j], crossed.at[j], c_send.at[j], c_recv.at[j], other)

    def arrived(s, j):
        sem = p_recv if s == 0 else g_recv.at[s]
        return remote(got.at[s, j], got.at[s, j], u_send, sem.at[j], other)

    def start_next(s, j):
        if s < n_shifts:
            pl.when(gives[s])(lambda: give(s + 1, j, shifts[s]).start())
        elif s == n_shifts:
            pl.when(gives_last)(lambda: give(s + 1, j, 1).start())

    for s in range(n_shifts + 1):
        slot = (s + 1) % 2

        @pl.when(takes[s])
        def _(s=s, slot=slot):
            if s > 0:
                def collect(j, _):
                    share(s - 1, j).wait_recv()
                    for k in range(2):
                        put(slot, 0, pl.multiple_of(theirs + j * WIDTH, WIDTH), k, swap[s - 1, j, k])
                    return 0

                lax.fori_loop(0, slabs, collect, 0)

            def take(j, _):
                arrived(s, j).wait_recv()
                x = got[s, j].reshape(2 * WIDTH, size)
                out = product(x, high[slot, 0], low[slot, 0])
                for k in range(2):
                    keep[s, 0, j, k] = out[k]
                start_next(s, j)
                if s < n_shifts:
                    share(s, j).start()
                    for k in range(2):
                        put(1 - slot, 0, pl.multiple_of(mine + j * WIDTH, WIDTH), k, out[k])
                return 0

            lax.fori_loop(0, slabs, take, 0)
            if s > 0:
                share_second(s - 1).wait_recv()
                for k in range(2):
                    put(slot, 1, theirs, k, swap_second[s - 1, :, k].reshape(half, size))
            out = product(stacked(got[s]), high[slot, 1], low[slot, 1])
            for k in range(2):
                keep[s, 1, :, k] = out[k].reshape(slabs, WIDTH, size)
            if s < n_shifts:
                share_second(s).start()
                for k in range(2):
                    put(1 - slot, 1, mine, k, out[k])

        if s > 0:
            @pl.when(jnp.logical_and(odd, jnp.logical_not(takes[s])))
            def _(s=s):
                if s > 0:
                    @pl.when(takes[s - 1])
                    def _():
                        def skip(j, _):
                            share(s - 1, j).wait_recv()
                            return 0

                        lax.fori_loop(0, slabs, skip, 0)
                        share_second(s - 1).wait_recv()

                def send(j, _):
                    start_next(s, j)
                    return 0

                lax.fori_loop(0, slabs, send, 0)

    def into_value(first, k, block):
        value[k, pl.ds(first, block.shape[0])] = block

    @pl.when(odd)
    def _():
        finish().start()
        for k in range(2):
            into_value(mine, k, keep[taken - 1, 1 - core, :, k].reshape(half, size))
        finish().wait_recv()
        for k in range(2):
            into_value(theirs, k, last[:, k].reshape(half, size))

    @pl.when(takes_last)
    def _():
        s = n_shifts + 1
        left_high, left_low = high.at[1, 1 - core], low.at[1, 1 - core]

        def take(j, _):
            arrived(s, j).wait_recv()
            cross(j).start()
            out = product(got[s, j].reshape(2 * WIDTH, size), left_high, left_low)
            for k in range(2):
                into_value(pl.multiple_of(mine + j * WIDTH, WIDTH), k, out[k])
            return 0

        lax.fori_loop(0, slabs, take, 0)
        for part in range(PARTS):
            for j in range(part * per_part, (part + 1) * per_part):
                cross(j).wait_recv()
            out = product(stacked(crossed[part * per_part:(part + 1) * per_part]), left_high, left_low)
            for k in range(2):
                into_value(pl.multiple_of(theirs + part * per_part * WIDTH, WIDTH), k, out[k])

    @pl.when(jnp.logical_and(chip == 0, first_core))
    def _():
        for k in range(2):
            into_value(0, k, unit[:, k].reshape(size, size))

    @pl.when(jnp.logical_and(chip == 0, second_core))
    def _():
        for part in range(PARTS):
            for side in range(2):
                for k in range(2):
                    block = total[part, side, :, k].reshape(half // PARTS, size)
                    into_value(side * half + part * (half // PARTS), k, block)

    o_ref[0] = value[0].T
    o_ref[1] = value[1].T

    h_copy.wait_send()
    pl.when(first_core)(lambda: u_copy.wait_send())

    @pl.when(jnp.logical_and(even, second_core))
    def _():
        for part in range(PARTS):
            for j in range(per_part):
                for side in range(2):
                    pair_give(part, side, j).wait_send()

    @pl.when(jnp.logical_and(odd, second_core))
    def _():
        for part in range(PARTS):
            total_copy(part).wait_send()

    @pl.when(odd)
    def _():
        def drain(j, _):
            for s in range(n_shifts):
                pl.when(gives[s])(lambda s=s: give(s + 1, j, shifts[s]).wait_send())
                pl.when(takes[s])(lambda s=s: share(s, j).wait_send())
            pl.when(gives_last)(lambda: give(n_shifts + 1, j, 1).wait_send())
            return 0

        lax.fori_loop(0, slabs, drain, 0)
        for s in range(n_shifts):
            pl.when(takes[s])(lambda s=s: share_second(s).wait_send())
        finish().wait_send()

    @pl.when(takes_last)
    def _():
        def drain(j, _):
            cross(j).wait_send()
            return 0

        lax.fori_loop(0, slabs, drain, 0)


def on_device(samples):
    x = samples[0]
    size = x.shape[-1]
    devices = lax.axis_size("tm")
    steps = (devices // 2).bit_length() - 1
    slabs = size // 2 // WIDTH
    f32, bf16 = jnp.float32, jnp.bfloat16
    slab = (2, WIDTH, size)
    dma = pltpu.SemaphoreType.DMA
    out = pl.pallas_call(
        functools.partial(kernel, devices),
        out_shape=jax.ShapeDtypeStruct(x.shape, f32),
        in_specs=[pl.BlockSpec(memory_space=pltpu.HBM)],
        out_specs=pl.BlockSpec(memory_space=pltpu.VMEM),
        scratch_shapes=[
            pltpu.VMEM((2, size, size), f32),
            pltpu.VMEM((size, size), f32),
            pltpu.VMEM((size, size), f32),
            pltpu.VMEM((2, size, size), f32),
            pltpu.VMEM((2 * slabs, *slab), f32),
            pltpu.VMEM((PARTS, 2, slabs // PARTS, *slab), f32),
            pltpu.VMEM((steps, 2, slabs, *slab), f32),
            pltpu.VMEM((steps + 1, slabs, *slab), f32),
            pltpu.VMEM((steps, slabs, *slab), f32),
            pltpu.VMEM((steps, slabs, *slab), f32),
            pltpu.VMEM((slabs, *slab), f32),
            pltpu.VMEM((slabs, *slab), f32),
            pltpu.VMEM((2, 2, 2, size, size), bf16),
            pltpu.VMEM((2, 2, 2, size, size), bf16),
            dma, dma, dma, dma, dma, dma((PARTS,)), dma((PARTS,)),
            dma((2, slabs)), dma((slabs,)),
            dma((steps + 1, slabs)), dma((steps + 1, slabs)),
            dma((steps, slabs)), dma((steps, slabs)),
            dma((steps,)), dma((steps,)),
            dma, dma, dma((slabs,)), dma((slabs,)),
        ],
        compiler_params=pltpu.CompilerParams(
            collective_id=0, has_side_effects=True, vmem_limit_bytes=48 << 20
        ),
        name="propagators",
    )(x)
    return out[None]


def solution(mesh):
    spec = P("tm", None, None, None)
    return jax.shard_map(on_device, mesh=mesh, in_specs=(spec,), out_specs=spec, check_vma=False)
```

```python
import functools

import jax
import jax.numpy as jnp
from jax import lax
from jax.experimental import pallas as pl
from jax.experimental.pallas import tpu as pltpu
from jax.sharding import PartitionSpec as P

MESH = pl.DeviceIdType.MESH
time_step = 0.25
WIDTH = 32
PARTS = 4


def halves(x):
    high = x.astype(jnp.bfloat16)
    return high, (x - high.astype(jnp.float32)).astype(jnp.bfloat16)


def dot(a, b):
    return jnp.dot(a, b, preferred_element_type=jnp.float32)


def product(x, high, low):
    m = x.shape[0]
    xh, xl = halves(x)
    both = jnp.concatenate([xh, xl], axis=0)
    by_real = dot(both, high[0])
    by_imag = dot(both, high[1])
    by_real = by_real[:m] + by_real[m:] + dot(xh, low[0])
    by_imag = by_imag[:m] + by_imag[m:] + dot(xh, low[1])
    n = m // 2
    return by_real[:n] - by_imag[n:], by_imag[:n] + by_real[n:]


def stacked(x):
    size = x.shape[-1]
    return jnp.concatenate([x[:, 0].reshape(-1, size), x[:, 1].reshape(-1, size)], axis=0)


def kernel(
    devices, x_ref, o_ref,
    drawn, packed, packed_in, value, unit, total, keep, got, swap, swap_second, last, crossed, high, low,
    x_sem, h_send, h_recv, u_send, u_recv, t_send, t_recv, p_send, p_recv, g_send, g_recv,
    s_send, s_recv, w_send, w_recv, f_send, f_recv, c_send, c_recv,
):
    size = x_ref.shape[-1]
    half = size // 2
    slabs = half // WIDTH
    per_part = slabs // PARTS
    chips = devices // 2
    me = lax.axis_index("tm")
    core = lax.rem(me, 2)
    chip = me // 2
    odd = lax.rem(chip, 2) == 1
    even = jnp.logical_not(odd)
    first_core = core == 0
    second_core = core == 1
    other = me + 1 - 2 * core
    before = lax.rem(me + devices - 1, devices)
    after = lax.rem(me + 1, devices)

    def device(chip, core):
        return chip * 2 + core

    shifts = []
    shift = 2
    while shift < chips:
        shifts.append(shift)
        shift *= 2
    n_shifts = len(shifts)
    takes = [odd] + [jnp.logical_and(odd, chip > by) for by in shifts]
    gives = [jnp.logical_and(odd, chip + by < chips) for by in shifts]
    gives_last = jnp.logical_and(odd, chip + 1 < chips)
    takes_last = jnp.logical_and(even, chip > 0)
    taken = sum(t.astype(jnp.int32) for t in takes)

    barrier = pltpu.get_barrier_semaphore()
    expected = 0

    def greet(when, device):
        @pl.when(when)
        def _():
            pl.semaphore_signal(barrier, inc=1, device_id=(device,), device_id_type=MESH)

        return when.astype(jnp.int32)

    always = chip >= 0
    pairs = [(always, other), (always, before), (always, after)]
    pairs += [(jnp.logical_and(even, second_core), device(chip + 1, c)) for c in range(2)]
    pairs += [(odd, device(chip - 1, 1))]
    for by, t, g in zip(shifts, takes[1:], gives):
        pairs += [(t, me - 2 * by), (g, me + 2 * by)]
    pairs += [(gives_last, me + 2), (takes_last, me - 2)]
    for when, where in pairs:
        expected = expected + greet(when, where)

    x_copy = pltpu.make_async_copy(x_ref, drawn, x_sem)
    x_copy.start()

    def remote(src, dst, send, recv, device):
        return pltpu.make_async_remote_copy(
            src_ref=src, dst_ref=dst, send_sem=send, recv_sem=recv,
            device_id=(device,), device_id_type=MESH,
        )

    row = lax.broadcasted_iota(jnp.int32, (size, size), 0)
    col = lax.broadcasted_iota(jnp.int32, (size, size), 1)
    x_copy.wait()
    h_real = (drawn[0] + drawn[0].T) * 0.5
    h_imag = (drawn[1] - drawn[1].T) * 0.5
    packed[...] = jnp.where(col >= row, h_real, h_imag)
    pl.semaphore_wait(barrier, expected)
    h_copy = remote(packed, packed_in, h_send, h_recv, before)
    h_copy.start()
    value[0] = h_real
    value[1] = h_imag
    for part, h in enumerate((h_real, h_imag)):
        high[0, 0, part], low[0, 0, part] = halves(h)
    h_copy.wait_recv()
    flat = packed_in[...]
    turned = flat.T
    n_real = jnp.where(col >= row, flat, turned)
    n_imag = jnp.where(row > col, flat, jnp.where(row < col, -turned, 0.0))
    x_real, x_imag = product(jnp.concatenate([n_real, n_imag], axis=0), high[0, 0], low[0, 0])
    shrink = time_step * time_step / 12.0
    m_real = shrink * (x_real - x_real.T) - 0.5 * time_step * (value[1] + n_imag)
    m_imag = -0.5 * time_step * (value[0] + n_real) - shrink * (x_imag + x_imag.T)
    for part, h in enumerate((m_real, m_imag)):
        high[0, 1, part], low[0, 1, part] = halves(h)

    def put(slot, which, first, part, value):
        rows = pl.ds(first, value.shape[0])
        high[slot, which, part, rows], low[slot, which, part, rows] = halves(value)

    u_copy = remote(unit, unit, u_send, u_recv, other)

    @pl.when(first_core)
    def _():
        eye = jnp.where(row == col, 1.0, 0.0)
        v_real = eye + m_real * 0.25
        v_imag = m_imag * 0.25
        for divisor in (3.0, 2.0, 1.0):
            v_real, v_imag = product(
                jnp.concatenate([v_real, v_imag], axis=0), high[0, 1], low[0, 1]
            )
            if divisor != 1.0:
                v_real = v_real * (1.0 / divisor)
                v_imag = v_imag * (1.0 / divisor)
            v_real = eye + v_real
        unit[:, 0] = v_real.reshape(2 * slabs, WIDTH, size)
        unit[:, 1] = v_imag.reshape(2 * slabs, WIDTH, size)
        u_copy.start()
        put(1, 1, 0, 0, v_real)
        put(1, 1, 0, 1, v_imag)

    def pair_give(part, side, j):
        slab = part * per_part + j
        return remote(
            total.at[part, side, j], got.at[0, slab], p_send.at[side, slab], p_recv.at[slab],
            device(chip + 1, side),
        )

    def total_copy(part):
        return remote(total.at[part], total.at[part], t_send.at[part], t_recv.at[part], other)

    @pl.when(second_core)
    def _():
        u_copy.wait_recv()
        def applied(y):
            z = y
            for divisor in (4.0, 3.0, 2.0, 1.0):
                z_real, z_imag = product(z, high[0, 1], low[0, 1])
                z = jnp.concatenate([z_real, z_imag], axis=0)
                if divisor != 1.0:
                    z = z * (1.0 / divisor)
                z = y + z
            return z

        @pl.when(odd)
        def _():
            z = applied(stacked(unit[...]))
            for k in range(2):
                block = z[k * size:(k + 1) * size].reshape(2, PARTS, per_part, WIDTH, size)
                for part in range(PARTS):
                    total[part, :, :, k] = block[:, part]
            for part in range(PARTS):
                total_copy(part).start()
            for k in range(2):
                put(1, 0, 0, k, z[k * size:(k + 1) * size])

        @pl.when(even)
        def _():
            for part in range(PARTS):
                sides = [
                    unit[side * slabs + part * per_part:side * slabs + (part + 1) * per_part]
                    for side in range(2)
                ]
                y = stacked(jnp.concatenate(sides, axis=0))
                rows = y.shape[0] // 2
                z = applied(y)
                for k in range(2):
                    block = z[k * rows:(k + 1) * rows]
                    total[part, :, :, k] = block.reshape(2, per_part, WIDTH, size)
                for j in range(per_part):
                    for side in range(2):
                        pair_give(part, side, j).start()
                for k in range(2):
                    for side in range(2):
                        first = k * rows + side * (rows // 2)
                        put(1, 0, side * half + part * (rows // 2), k, z[first:first + rows // 2])

        @pl.when(odd)
        def _():
            for k in range(2):
                put(1, 1, 0, k, unit[:, k].reshape(size, size))

    @pl.when(jnp.logical_and(odd, first_core))
    def _():
        for part in range(PARTS):
            total_copy(part).wait_recv()
            for side in range(2):
                for k in range(2):
                    block = total[part, side, :, k].reshape(half // PARTS, size)
                    put(1, 0, side * half + part * (half // PARTS), k, block)

    mine = pl.multiple_of(core * half, half)
    theirs = pl.multiple_of((1 - core) * half, half)

    def give(s, j, by):
        return remote(
            keep.at[jnp.minimum(s, taken) - 1, 0, j], got.at[s, j], g_send.at[s, j], g_recv.at[s, j],
            me + 2 * by,
        )

    def share(s, j):
        return remote(keep.at[s, 0, j], swap.at[s, j], s_send.at[s, j], s_recv.at[s, j], other)

    def share_second(s):
        return remote(keep.at[s, 1], swap_second.at[s], w_send.at[s], w_recv.at[s], other)

    def finish():
        return remote(keep.at[taken - 1, core], last, f_send, f_recv, other)

    def cross(j):
        return remote(got.at[n_shifts + 1, j], crossed.at[j], c_send.at[j], c_recv.at[j], other)

    def arrived(s, j):
        sem = p_recv if s == 0 else g_recv.at[s]
        return remote(got.at[s, j], got.at[s, j], u_send, sem.at[j], other)

    def start_next(s, j):
        if s < n_shifts:
            pl.when(gives[s])(lambda: give(s + 1, j, shifts[s]).start())
        elif s == n_shifts:
            pl.when(gives_last)(lambda: give(s + 1, j, 1).start())

    for s in range(n_shifts + 1):
        slot = (s + 1) % 2

        @pl.when(takes[s])
        def _(s=s, slot=slot):
            if s > 0:
                def collect(j, _):
                    share(s - 1, j).wait_recv()
                    for k in range(2):
                        put(slot, 0, pl.multiple_of(theirs + j * WIDTH, WIDTH), k, swap[s - 1, j, k])
                    return 0

                lax.fori_loop(0, slabs, collect, 0)

            def take(j, _):
                arrived(s, j).wait_recv()
                x = got[s, j].reshape(2 * WIDTH, size)
                out = product(x, high[slot, 0], low[slot, 0])
                for k in range(2):
                    keep[s, 0, j, k] = out[k]
                start_next(s, j)
                if s < n_shifts:
                    share(s, j).start()
                    for k in range(2):
                        put(1 - slot, 0, pl.multiple_of(mine + j * WIDTH, WIDTH), k, out[k])
                return 0

            lax.fori_loop(0, slabs, take, 0)
            if s > 0:
                share_second(s - 1).wait_recv()
                for k in range(2):
                    put(slot, 1, theirs, k, swap_second[s - 1, :, k].reshape(half, size))
            out = product(stacked(got[s]), high[slot, 1], low[slot, 1])
            for k in range(2):
                keep[s, 1, :, k] = out[k].reshape(slabs, WIDTH, size)
            if s < n_shifts:
                share_second(s).start()
                for k in range(2):
                    put(1 - slot, 1, mine, k, out[k])

        if s > 0:
            @pl.when(jnp.logical_and(odd, jnp.logical_not(takes[s])))
            def _(s=s):
                if s > 0:
                    @pl.when(takes[s - 1])
                    def _():
                        def skip(j, _):
                            share(s - 1, j).wait_recv()
                            return 0

                        lax.fori_loop(0, slabs, skip, 0)
                        share_second(s - 1).wait_recv()

                def send(j, _):
                    start_next(s, j)
                    return 0

                lax.fori_loop(0, slabs, send, 0)

    def into_value(first, k, block):
        value[k, pl.ds(first, block.shape[0])] = block

    @pl.when(odd)
    def _():
        finish().start()
        for k in range(2):
            into_value(mine, k, keep[taken - 1, 1 - core, :, k].reshape(half, size))
        finish().wait_recv()
        for k in range(2):
            into_value(theirs, k, last[:, k].reshape(half, size))

    @pl.when(takes_last)
    def _():
        s = n_shifts + 1
        left_high, left_low = high.at[1, 1 - core], low.at[1, 1 - core]

        def take(j, _):
            arrived(s, j).wait_recv()
            cross(j).start()
            out = product(got[s, j].reshape(2 * WIDTH, size), left_high, left_low)
            for k in range(2):
                into_value(pl.multiple_of(mine + j * WIDTH, WIDTH), k, out[k])
            return 0

        lax.fori_loop(0, slabs, take, 0)
        for part in range(PARTS):
            for j in range(part * per_part, (part + 1) * per_part):
                cross(j).wait_recv()
            out = product(stacked(crossed[part * per_part:(part + 1) * per_part]), left_high, left_low)
            for k in range(2):
                into_value(pl.multiple_of(theirs + part * per_part * WIDTH, WIDTH), k, out[k])

    @pl.when(jnp.logical_and(chip == 0, first_core))
    def _():
        for k in range(2):
            into_value(0, k, unit[:, k].reshape(size, size))

    @pl.when(jnp.logical_and(chip == 0, second_core))
    def _():
        for part in range(PARTS):
            for side in range(2):
                for k in range(2):
                    block = total[part, side, :, k].reshape(half // PARTS, size)
                    into_value(side * half + part * (half // PARTS), k, block)

    o_ref[0] = value[0].T
    o_ref[1] = value[1].T

    h_copy.wait_send()
    pl.when(first_core)(lambda: u_copy.wait_send())

    @pl.when(jnp.logical_and(even, second_core))
    def _():
        for part in range(PARTS):
            for j in range(per_part):
                for side in range(2):
                    pair_give(part, side, j).wait_send()

    @pl.when(jnp.logical_and(odd, second_core))
    def _():
        for part in range(PARTS):
            total_copy(part).wait_send()

    @pl.when(odd)
    def _():
        def drain(j, _):
            for s in range(n_shifts):
                pl.when(gives[s])(lambda s=s: give(s + 1, j, shifts[s]).wait_send())
                pl.when(takes[s])(lambda s=s: share(s, j).wait_send())
            pl.when(gives_last)(lambda: give(n_shifts + 1, j, 1).wait_send())
            return 0

        lax.fori_loop(0, slabs, drain, 0)
        for s in range(n_shifts):
            pl.when(takes[s])(lambda s=s: share_second(s).wait_send())
        finish().wait_send()

    @pl.when(takes_last)
    def _():
        def drain(j, _):
            cross(j).wait_send()
            return 0

        lax.fori_loop(0, slabs, drain, 0)


def on_device(samples):
    x = samples[0]
    size = x.shape[-1]
    devices = lax.axis_size("tm")
    steps = (devices // 2).bit_length() - 1
    slabs = size // 2 // WIDTH
    f32, bf16 = jnp.float32, jnp.bfloat16
    slab = (2, WIDTH, size)
    dma = pltpu.SemaphoreType.DMA
    out = pl.pallas_call(
        functools.partial(kernel, devices),
        out_shape=jax.ShapeDtypeStruct(x.shape, f32),
        in_specs=[pl.BlockSpec(memory_space=pltpu.HBM)],
        out_specs=pl.BlockSpec(memory_space=pltpu.VMEM),
        scratch_shapes=[
            pltpu.VMEM((2, size, size), f32),
            pltpu.VMEM((size, size), f32),
            pltpu.VMEM((size, size), f32),
            pltpu.VMEM((2, size, size), f32),
            pltpu.VMEM((2 * slabs, *slab), f32),
            pltpu.VMEM((PARTS, 2, slabs // PARTS, *slab), f32),
            pltpu.VMEM((steps, 2, slabs, *slab), f32),
            pltpu.VMEM((steps + 1, slabs, *slab), f32),
            pltpu.VMEM((steps, slabs, *slab), f32),
            pltpu.VMEM((steps, slabs, *slab), f32),
            pltpu.VMEM((slabs, *slab), f32),
            pltpu.VMEM((slabs, *slab), f32),
            pltpu.VMEM((2, 2, 2, size, size), bf16),
            pltpu.VMEM((2, 2, 2, size, size), bf16),
            dma, dma, dma, dma, dma, dma((PARTS,)), dma((PARTS,)),
            dma((2, slabs)), dma((slabs,)),
            dma((steps + 1, slabs)), dma((steps + 1, slabs)),
            dma((steps, slabs)), dma((steps, slabs)),
            dma((steps,)), dma((steps,)),
            dma, dma, dma((slabs,)), dma((slabs,)),
        ],
        compiler_params=pltpu.CompilerParams(
            collective_id=0, has_side_effects=True, vmem_limit_bytes=48 << 20
        ),
        name="propagators",
    )(x)
    return out[None]


def solution(mesh):
    spec = P("tm", None, None, None)
    return jax.shard_map(on_device, mesh=mesh, in_specs=(spec,), out_specs=spec, check_vma=False)
```

```python
import functools

import jax
import jax.numpy as jnp
from jax import lax
from jax.experimental import pallas as pl
from jax.experimental.pallas import tpu as pltpu
from jax.sharding import PartitionSpec as P

MESH = pl.DeviceIdType.MESH
time_step = 0.25
WIDTH = 32
PARTS = 4


def halves(x):
    high = x.astype(jnp.bfloat16)
    return high, (x - high.astype(jnp.float32)).astype(jnp.bfloat16)


def dot(a, b):
    return jnp.dot(a, b, preferred_element_type=jnp.float32)


def product(x, high, low):
    m = x.shape[0]
    xh, xl = halves(x)
    both = jnp.concatenate([xh, xl], axis=0)
    by_real = dot(both, high[0])
    by_imag = dot(both, high[1])
    by_real = by_real[:m] + by_real[m:] + dot(xh, low[0])
    by_imag = by_imag[:m] + by_imag[m:] + dot(xh, low[1])
    n = m // 2
    return by_real[:n] - by_imag[n:], by_imag[:n] + by_real[n:]


def stacked(x):
    size = x.shape[-1]
    return jnp.concatenate([x[:, 0].reshape(-1, size), x[:, 1].reshape(-1, size)], axis=0)


def kernel(
    devices, x_ref, o_ref,
    drawn, packed, packed_in, value, unit, total, keep, got, swap, swap_second, last, high, low,
    x_sem, h_send, h_recv, u_send, u_recv, t_send, t_recv, p_send, p_recv, g_send, g_recv,
    s_send, s_recv, w_send, w_recv, f_send, f_recv,
):
    size = x_ref.shape[-1]
    half = size // 2
    slabs = half // WIDTH
    per_part = slabs // PARTS
    chips = devices // 2
    me = lax.axis_index("tm")
    core = lax.rem(me, 2)
    chip = me // 2
    first_core = core == 0
    second_core = core == 1
    other = me + 1 - 2 * core
    before = lax.rem(me + devices - 1, devices)
    after = lax.rem(me + 1, devices)

    def device(chip, core):
        return chip * 2 + core

    shifts = []
    shift = 2
    while shift < chips:
        shifts.append(shift)
        shift *= 2
    n_shifts = len(shifts)
    takes = [chip >= by for by in [1] + shifts]
    gives_first = chip + 1 < chips
    gives = [chip + by < chips for by in shifts]
    taken = jnp.maximum(sum(t.astype(jnp.int32) for t in takes), 1)

    barrier = pltpu.get_barrier_semaphore()
    expected = 0

    def greet(when, device):
        @pl.when(when)
        def _():
            pl.semaphore_signal(barrier, inc=1, device_id=(device,), device_id_type=MESH)

        return when.astype(jnp.int32)

    always = chip >= 0
    pairs = [(always, other), (always, before), (always, after)]
    pairs += [(jnp.logical_and(gives_first, second_core), device(chip + 1, c)) for c in range(2)]
    pairs += [(takes[0], device(chip - 1, 1))]
    for by, t, g in zip(shifts, takes[1:], gives):
        pairs += [(t, me - 2 * by), (g, me + 2 * by)]
    for when, where in pairs:
        expected = expected + greet(when, where)

    x_copy = pltpu.make_async_copy(x_ref, drawn, x_sem)
    x_copy.start()

    def remote(src, dst, send, recv, device):
        return pltpu.make_async_remote_copy(
            src_ref=src, dst_ref=dst, send_sem=send, recv_sem=recv,
            device_id=(device,), device_id_type=MESH,
        )

    row = lax.broadcasted_iota(jnp.int32, (size, size), 0)
    col = lax.broadcasted_iota(jnp.int32, (size, size), 1)
    x_copy.wait()
    h_real = (drawn[0] + drawn[0].T) * 0.5
    h_imag = (drawn[1] - drawn[1].T) * 0.5
    packed[...] = jnp.where(col >= row, h_real, h_imag)
    pl.semaphore_wait(barrier, expected)
    h_copy = remote(packed, packed_in, h_send, h_recv, before)
    h_copy.start()
    value[0] = h_real
    value[1] = h_imag
    for part, h in enumerate((h_real, h_imag)):
        high[0, 0, part], low[0, 0, part] = halves(h)
    h_copy.wait_recv()
    flat = packed_in[...]
    turned = flat.T
    n_real = jnp.where(col >= row, flat, turned)
    n_imag = jnp.where(row > col, flat, jnp.where(row < col, -turned, 0.0))
    x_real, x_imag = product(jnp.concatenate([n_real, n_imag], axis=0), high[0, 0], low[0, 0])
    shrink = time_step * time_step / 12.0
    m_real = shrink * (x_real - x_real.T) - 0.5 * time_step * (value[1] + n_imag)
    m_imag = -0.5 * time_step * (value[0] + n_real) - shrink * (x_imag + x_imag.T)
    for part, h in enumerate((m_real, m_imag)):
        high[0, 1, part], low[0, 1, part] = halves(h)

    def put(slot, which, first, part, value):
        rows = pl.ds(first, value.shape[0])
        high[slot, which, part, rows], low[slot, which, part, rows] = halves(value)

    u_copy = remote(unit, unit, u_send, u_recv, other)

    @pl.when(first_core)
    def _():
        eye = jnp.where(row == col, 1.0, 0.0)
        v_real = eye + m_real * 0.25
        v_imag = m_imag * 0.25
        for divisor in (3.0, 2.0, 1.0):
            v_real, v_imag = product(
                jnp.concatenate([v_real, v_imag], axis=0), high[0, 1], low[0, 1]
            )
            if divisor != 1.0:
                v_real = v_real * (1.0 / divisor)
                v_imag = v_imag * (1.0 / divisor)
            v_real = eye + v_real
        unit[:, 0] = v_real.reshape(2 * slabs, WIDTH, size)
        unit[:, 1] = v_imag.reshape(2 * slabs, WIDTH, size)
        u_copy.start()
        put(1, 1, 0, 0, v_real)
        put(1, 1, 0, 1, v_imag)

    def pair_give(part, side, j):
        slab = part * per_part + j
        return remote(
            total.at[part, side, j], got.at[0, slab], p_send.at[side, slab], p_recv.at[slab],
            device(chip + 1, side),
        )

    def total_copy(part):
        return remote(total.at[part], total.at[part], t_send.at[part], t_recv.at[part], other)

    @pl.when(second_core)
    def _():
        u_copy.wait_recv()
        def applied(y):
            z = y
            for divisor in (4.0, 3.0, 2.0, 1.0):
                z_real, z_imag = product(z, high[0, 1], low[0, 1])
                z = jnp.concatenate([z_real, z_imag], axis=0)
                if divisor != 1.0:
                    z = z * (1.0 / divisor)
                z = y + z
            return z

        for part in range(PARTS):
            sides = [
                unit[side * slabs + part * per_part:side * slabs + (part + 1) * per_part]
                for side in range(2)
            ]
            y = stacked(jnp.concatenate(sides, axis=0))
            rows = y.shape[0] // 2
            z = applied(y)
            for k in range(2):
                block = z[k * rows:(k + 1) * rows]
                total[part, :, :, k] = block.reshape(2, per_part, WIDTH, size)
            @pl.when(gives_first)
            def _(part=part):
                for j in range(per_part):
                    for side in range(2):
                        pair_give(part, side, j).start()

            total_copy(part).start()
            for k in range(2):
                for side in range(2):
                    first = k * rows + side * (rows // 2)
                    put(1, 0, side * half + part * (rows // 2), k, z[first:first + rows // 2])

        for k in range(2):
            put(1, 1, 0, k, unit[:, k].reshape(size, size))

    @pl.when(first_core)
    def _():
        for part in range(PARTS):
            total_copy(part).wait_recv()
            for side in range(2):
                for k in range(2):
                    block = total[part, side, :, k].reshape(half // PARTS, size)
                    put(1, 0, side * half + part * (half // PARTS), k, block)

    mine = pl.multiple_of(core * half, half)
    theirs = pl.multiple_of((1 - core) * half, half)

    def give(s, j, by):
        return remote(
            keep.at[jnp.minimum(s, taken) - 1, 0, j], got.at[s, j], g_send.at[s, j], g_recv.at[s, j],
            me + 2 * by,
        )

    def share(s, j):
        return remote(keep.at[s, 0, j], swap.at[s, j], s_send.at[s, j], s_recv.at[s, j], other)

    def share_second(s):
        return remote(keep.at[s, 1], swap_second.at[s], w_send.at[s], w_recv.at[s], other)

    def finish():
        return remote(keep.at[taken - 1, core], last, f_send, f_recv, other)

    def arrived(s, j):
        sem = p_recv if s == 0 else g_recv.at[s]
        return remote(got.at[s, j], got.at[s, j], u_send, sem.at[j], other)

    def start_next(s, j):
        if s < n_shifts:
            pl.when(gives[s])(lambda: give(s + 1, j, shifts[s]).start())

    for s in range(n_shifts + 1):
        slot = (s + 1) % 2

        @pl.when(takes[s])
        def _(s=s, slot=slot):
            if s > 0:
                def collect(j, _):
                    share(s - 1, j).wait_recv()
                    for k in range(2):
                        put(slot, 0, pl.multiple_of(theirs + j * WIDTH, WIDTH), k, swap[s - 1, j, k])
                    return 0

                lax.fori_loop(0, slabs, collect, 0)

            def take(j, _):
                arrived(s, j).wait_recv()
                x = got[s, j].reshape(2 * WIDTH, size)
                out = product(x, high[slot, 0], low[slot, 0])
                for k in range(2):
                    keep[s, 0, j, k] = out[k]
                start_next(s, j)
                if s < n_shifts:
                    share(s, j).start()
                    for k in range(2):
                        put(1 - slot, 0, pl.multiple_of(mine + j * WIDTH, WIDTH), k, out[k])
                return 0

            lax.fori_loop(0, slabs, take, 0)
            if s > 0:
                share_second(s - 1).wait_recv()
                for k in range(2):
                    put(slot, 1, theirs, k, swap_second[s - 1, :, k].reshape(half, size))
            out = product(stacked(got[s]), high[slot, 1], low[slot, 1])
            for k in range(2):
                keep[s, 1, :, k] = out[k].reshape(slabs, WIDTH, size)
            if s < n_shifts:
                share_second(s).start()
                for k in range(2):
                    put(1 - slot, 1, mine, k, out[k])

        @pl.when(jnp.logical_not(takes[s]))
        def _(s=s):
            if s > 0:
                @pl.when(takes[s - 1])
                def _():
                    def skip(j, _):
                        share(s - 1, j).wait_recv()
                        return 0

                    lax.fori_loop(0, slabs, skip, 0)
                    share_second(s - 1).wait_recv()

            if s == 0:
                for part in range(PARTS):
                    span = slice(part * per_part, (part + 1) * per_part)
                    keep[0, 0, span] = total[part, core]
                keep[0, 1] = unit[pl.ds(core * slabs, slabs)]

            def send(j, _):
                start_next(s, j)
                return 0

            lax.fori_loop(0, slabs, send, 0)

    def into_value(first, k, block):
        value[k, pl.ds(first, block.shape[0])] = block

    finish().start()
    for k in range(2):
        into_value(mine, k, keep[taken - 1, 1 - core, :, k].reshape(half, size))
    finish().wait_recv()
    for k in range(2):
        into_value(theirs, k, last[:, k].reshape(half, size))

    o_ref[0] = value[0].T
    o_ref[1] = value[1].T

    h_copy.wait_send()
    pl.when(first_core)(lambda: u_copy.wait_send())

    @pl.when(jnp.logical_and(gives_first, second_core))
    def _():
        for part in range(PARTS):
            for j in range(per_part):
                for side in range(2):
                    pair_give(part, side, j).wait_send()

    @pl.when(second_core)
    def _():
        for part in range(PARTS):
            total_copy(part).wait_send()

    @pl.when(always)
    def _():
        def drain(j, _):
            for s in range(n_shifts):
                pl.when(gives[s])(lambda s=s: give(s + 1, j, shifts[s]).wait_send())
                pl.when(takes[s])(lambda s=s: share(s, j).wait_send())
            return 0

        lax.fori_loop(0, slabs, drain, 0)
        for s in range(n_shifts):
            pl.when(takes[s])(lambda s=s: share_second(s).wait_send())
        finish().wait_send()


def on_device(samples):
    x = samples[0]
    size = x.shape[-1]
    devices = lax.axis_size("tm")
    steps = (devices // 2).bit_length() - 1
    slabs = size // 2 // WIDTH
    f32, bf16 = jnp.float32, jnp.bfloat16
    slab = (2, WIDTH, size)
    dma = pltpu.SemaphoreType.DMA
    out = pl.pallas_call(
        functools.partial(kernel, devices),
        out_shape=jax.ShapeDtypeStruct(x.shape, f32),
        in_specs=[pl.BlockSpec(memory_space=pltpu.HBM)],
        out_specs=pl.BlockSpec(memory_space=pltpu.VMEM),
        scratch_shapes=[
            pltpu.VMEM((2, size, size), f32),
            pltpu.VMEM((size, size), f32),
            pltpu.VMEM((size, size), f32),
            pltpu.VMEM((2, size, size), f32),
            pltpu.VMEM((2 * slabs, *slab), f32),
            pltpu.VMEM((PARTS, 2, slabs // PARTS, *slab), f32),
            pltpu.VMEM((steps, 2, slabs, *slab), f32),
            pltpu.VMEM((steps + 1, slabs, *slab), f32),
            pltpu.VMEM((steps, slabs, *slab), f32),
            pltpu.VMEM((steps, slabs, *slab), f32),
            pltpu.VMEM((slabs, *slab), f32),
            pltpu.VMEM((2, 2, 2, size, size), bf16),
            pltpu.VMEM((2, 2, 2, size, size), bf16),
            dma, dma, dma, dma, dma, dma((PARTS,)), dma((PARTS,)),
            dma((2, slabs)), dma((slabs,)),
            dma((steps + 1, slabs)), dma((steps + 1, slabs)),
            dma((steps, slabs)), dma((steps, slabs)),
            dma((steps,)), dma((steps,)),
            dma, dma,
        ],
        compiler_params=pltpu.CompilerParams(
            collective_id=0, has_side_effects=True, vmem_limit_bytes=48 << 20
        ),
        name="propagators",
    )(x)
    return out[None]


def solution(mesh):
    spec = P("tm", None, None, None)
    return jax.shard_map(on_device, mesh=mesh, in_specs=(spec,), out_specs=spec, check_vma=False)
```
